512 devices in a mesh: row: 16 (over y, z_hi), col: 32 (over x, z_lo, core).
Axes of the slice: x: 4, y: 4, z: 16 (z_hi: 4, z_lo: 4; z = z_hi * 4 + z_lo), core: 2. Of those that a mesh axis runs over, the one named last changes fastest.
Arguments:
- factor: float32 [8, 16, 128, 4, 32, 128], P(None, 'row', None, None, 'col'), may hold values from -0.0234375 to 0.0234375
- diag_inverse: float32 [4, 1, 32, 128, 2, 16, 128], P(None, None, 'col', None, None, 'row'), may hold values from -1 to 2
- right_side: float32 [4, 32, 128, 512], P(None, 'col'), may hold values from -6 to 6
Outputs:
- solution: float32 [8, 16, 128, 512], P(None, 'row')
The draws below stay inside these ranges and needn't reach their ends.
All inputs are finite; a program needn't handle non-finite values.
Results may differ from the reference program's by a relative error of at most 0.0001.
Values sent between devices are 32-bit elements; how exact they have to be, the bound alone decides.
A program may use at most 64 MiB of HBM per device.

```python
import math
import jax
import jax.numpy as jnp
from jax import lax

N = 16384
NP = 4
NB = 128
K = 512
PB = 4096
LI = 8
LJ = 4
BJ = 1
AI = 2
N_ROW = 16
N_COL = 32


def draw_diag_inverse(key, part):
    key = jax.random.fold_in(key, 7)
    noise = jnp.clip(jax.random.normal(key, (NP, PB, PB), jnp.float32), -4.0, 4.0)
    identity = (lax.broadcasted_iota(jnp.int32, (PB, PB), 0) == lax.broadcasted_iota(jnp.int32, (PB, PB), 1)).astype(jnp.float32)
    dense = identity[None] + noise * (0.5 / math.sqrt(PB))
    return dense.reshape(NP, BJ, N_COL, NB, AI, N_ROW, NB)


def block_scale(rng, shape, split, least, top_value):
    loudness = 1.0
    for position, shards_of in split:
        heights = jax.random.uniform(jax.random.fold_in(jax.random.fold_in(rng, 6), position), (shards_of,), jnp.float32, least / len(split), top_value / len(split))
        loudness = loudness * jnp.repeat(jnp.exp(heights), shape[position] // shards_of).reshape((-1,) + (1,) * (len(shape) - 1 - position))
    return loudness


def centred(key, extent, scale, most, shards=(), held_as=jnp.bfloat16):
    result = jax.random.normal(key, extent, jnp.float32) * scale
    if len(shards) > 0:
        result = block_scale(key, extent, shards, -0.22, 0.18) * result
    return jnp.clip(result, min=-most, max=most).astype(held_as)


def setup_inputs(seed: int = 0) -> dict:
    splits = jax.random.split(jax.random.key(seed), 4)
    factor = centred(splits[0], (LI, N_ROW, NB, LJ, N_COL, NB), (4 * N) ** -0.5, 0.0234375, ((1, 16), (4, 32)), jnp.float32)
    diag_inverse = draw_diag_inverse(jax.random.fold_in(splits[3], 71), 0)
    right_side = centred(splits[2], (LJ, N_COL, NB, K), 1.0, 6.0, ((1, 32),), jnp.float32)
    return {"factor": factor, "diag_inverse": diag_inverse, "right_side": right_side}


def reference(factor, diag_inverse, right_side):
    factor_full = factor.reshape(N, N)
    blocks = diag_inverse.reshape(NP, PB, PB)
    targets = right_side.reshape(N, K)
    solved = []
    for step_index in range(NP):
        current = targets[step_index * PB:(step_index + 1) * PB]
        if step_index > 0:
            earlier = jnp.concatenate(solved, axis=0)
            panel_part = factor_full[:step_index * PB, step_index * PB:(step_index + 1) * PB]
            update = jnp.dot(panel_part.T, earlier, precision=lax.Precision.HIGHEST, preferred_element_type=jnp.float32)
            current = current - update
        solved.append(jnp.dot(blocks[step_index].T, current, precision=lax.Precision.HIGHEST, preferred_element_type=jnp.float32))
    solution = jnp.concatenate(solved, axis=0)
    return solution.reshape(LI, N_ROW, NB, K)
```

```python
import functools

import jax
import jax.numpy as jnp
from jax import lax
from jax.experimental import pallas as pl
from jax.experimental.pallas import tpu as pltpu
from jax.sharding import PartitionSpec as P

F32 = jnp.float32
BF16 = jnp.bfloat16
MESH = pl.DeviceIdType.MESH
NC = 2
KS = 64
KC = KS // NC
YC = KC // 4
PAIRS = ((0, 1), (0, 2), (1, 2), (0, 3), (1, 3), (2, 3))
BLOCK = {pair: index for index, pair in enumerate(PAIRS)}


def split(value):
    high = value.astype(BF16)
    return high, (value - high.astype(F32)).astype(BF16)


def dot3(high, low, right_high, right_low):
    rows = high.shape[0]
    both = jnp.dot(
        jnp.concatenate([high, low], axis=0), right_high, preferred_element_type=F32
    )
    cross = jnp.dot(high, right_low, preferred_element_type=F32)
    return both[:rows] + (both[rows:] + cross)


def kernel(
    fac, dinv, rhs, out,
    facv, dinvv, bv, bT, bS, bR,
    Uall, Dall, Uh, Ul, Dh, Dl,
    P0, Rc, Rx, Z, CT, Ry, H, CY, X, OT,
    lsem, ssem, rsem,
):
    row = lax.axis_index("row")
    col = lax.axis_index("col")
    y, zh = row // 4, lax.rem(row, 4)
    x, zl, co = col // 8, lax.rem(col // 2, 4), lax.rem(col, 2)

    def dev(y_, zh_, x_, zl_, co_):
        return (y_ * 4 + zh_, (x_ * 4 + zl_) * 2 + co_)

    ring = lambda at, k: lax.rem(at + k, 4)
    core_peer = dev(y, zh, x, zl, 1 - co)
    x_peer = {k: dev(y, zh, ring(x, k), zl, co) for k in (1, 2, 3)}
    xc_peer = {k: dev(y, zh, ring(x, k), zl, 1 - co) for k in (1, 2, 3)}
    y_peer = {k: dev(ring(y, k), zh, x, zl, co) for k in (1, 2, 3)}
    zh_peer = {k: dev(y, ring(zh, k), x, zl, co) for k in (1, 2, 3)}
    zl_peer = {k: dev(y, zh, x, ring(zl, k), co) for k in (1, 2, 3)}
    order = (2, 1, 3)

    started = []

    def send(src, dst, peer):
        index = len(started)
        copy = pltpu.make_async_remote_copy(
            src_ref=src, dst_ref=dst, send_sem=ssem.at[index], recv_sem=rsem.at[index],
            device_id=peer, device_id_type=MESH,
        )
        copy.start()
        started.append(copy)
        return copy

    def arrive(copies):
        for copy in copies:
            copy.wait_recv()

    loads = [
        pltpu.make_async_copy(dinv, dinvv, lsem.at[0]),
        pltpu.make_async_copy(rhs, bv, lsem.at[1]),
        pltpu.make_async_copy(fac.at[pl.ds(0, 3072)], facv, lsem.at[2]),
    ]
    for copy in loads:
        copy.start()
    barrier = pltpu.get_barrier_semaphore()
    greeted = [core_peer]
    for group in (x_peer, xc_peer, y_peer, zh_peer, zl_peer):
        greeted += [group[k] for k in order]
    for peer in greeted:
        pl.semaphore_signal(barrier, inc=1, device_id=peer, device_id_type=MESH)

    loads[0].wait()
    loads[1].wait()
    d0 = jnp.concatenate(
        [dinvv[pl.ds(a, 128, stride=2), :] for a in range(2)], axis=1
    )
    d0h, d0l = split(d0)
    b0h, b0l = split(bv[0].T)
    for half in range(2):
        for quarter in range(4):
            at = 256 * half + 64 * quarter
            value = dot3(b0h[at : at + 64], b0l[at : at + 64], d0h, d0l)
            for ch in range(NC):
                P0[half, ch, quarter] = value[ch * KC : (ch + 1) * KC]

    loads[2].wait()
    for (q, p), block in BLOCK.items():
        Uall[block, 0, 0] = facv[pl.ds(1024 * q + p, 256, stride=4), :]
    for p in range(1, 4):
        for a in range(2):
            Dall[p - 1, 0, 0, :, a * 128 : (a + 1) * 128] = dinvv[
                pl.ds(256 * p + a, 128, stride=2), :
            ]

    pl.semaphore_wait(barrier, len(greeted))

    core_copies = [
        send(P0.at[1 - co, ch], Rc.at[ch], core_peer) for ch in range(NC)
    ]

    for p in range(1, 4):
        bT[p - 1] = bv[p].T
    for dco in range(2):
        for dx in range(4):
            to_co = co if dco == 0 else 1 - co
            base = 256 * to_co + 64 * ring(x, dx) + YC * y
            for p in range(3):
                for ch in range(NC):
                    at = pl.multiple_of(base + KC * ch, 8)
                    piece = bT[p, pl.ds(at, YC), :]
                    if dco == 0 and dx == 0:
                        bR[0, p, ch] = piece
                    else:
                        bS[dco * 4 + dx, p, ch] = piece

    def spread(buffer, block):
        return [
            send(buffer.at[block, 0, 0], buffer.at[block, 0, k], x_peer[k]) for k in order
        ]

    def forward(buffer, block, copies):
        arrive(copies)
        return [send(buffer.at[block, 0], buffer.at[block, 1], core_peer)]

    def ready_u(block, copies):
        arrive(copies)

        def body(slot, carry):
            high, low = split(Uall[block, slot // 4, lax.rem(slot, 4)])
            lanes = pl.ds(pl.multiple_of(slot * 128, 128), 128)
            Uh[block, :, lanes] = high
            Ul[block, :, lanes] = low
            return carry

        lax.fori_loop(0, 8, body, 0)

    def ready_d(block, copies):
        arrive(copies)

        def body(slot, carry):
            high, low = split(Dall[block, slot // 4, lax.rem(slot, 4)])
            rows = pl.ds(pl.multiple_of(slot * 128, 128), 128)
            Dh[block, rows, :] = high
            Dl[block, rows, :] = low
            return carry

        lax.fori_loop(0, 8, body, 0)

    def share(buffer, me, peers):
        return [send(buffer.at[me], buffer.at[me], peers[k]) for k in order]

    def total(buffer):
        return (buffer[0] + buffer[1]) + (buffer[2] + buffer[3])

    x_copies = []
    for ch in range(NC):
        arrive(core_copies[ch : ch + 1])
        P0[co, ch] = P0[co, ch] + Rc[ch]
        x_copies.append(
            [send(P0.at[co, ch, ring(x, k)], Rx.at[ch, k - 1], x_peer[k]) for k in order]
        )
    b_copies = []
    for dco in range(2):
        for dx in range(4):
            if dco or dx:
                peer = (x_peer[dx] if dco == 0 else core_peer if dx == 0 else xc_peer[dx])
                b_copies.append(send(bS.at[dco * 4 + dx], bR.at[dco * 4 + dx], peer))
    u01 = spread(Uall, 0)
    z_copies = []
    for ch in range(NC):
        arrive(x_copies[ch])
        Z[0, ch, zl] = (P0[co, ch, x] + Rx[ch, 0]) + (Rx[ch, 1] + Rx[ch, 2])
        z_copies.append(share(Z.at[0, ch], zl, zl_peer))
    d1 = spread(Dall, 0)
    ready_u(0, forward(Uall, 0, u01))

    def add_update(p, q, first, count):
        block = BLOCK[(q, p)]
        high, low = split(X[q, pl.ds(first, count), :])
        for n in range(4):
            lanes = slice(256 * n, 256 * (n + 1))
            value = dot3(high, low, Uh[block, :, lanes], Ul[block, :, lanes])
            if q > 0:
                value = value + CT[p - 1, pl.ds(first, count), lanes]
            CT[p - 1, pl.ds(first, count), lanes] = value

    out_first = {}
    out_second = {}
    stores = []

    def output_first(p):
        OT[p, co, x] = X[p]
        out_first[p] = [
            send(OT.at[p, co, x], OT.at[p, co, x], x_peer[k]) for k in order
        ]

    def output_second(p):
        arrive(out_first[p])
        out_second[p] = [send(OT.at[p, co], OT.at[p, co], core_peer)]

    def output_third(p):
        arrive(out_second[p])
        copy = pltpu.make_async_copy(OT.at[p], out.at[p], lsem.at[3 + p])
        copy.start()
        stores.append(copy)

    pending = {}
    for p in range(1, 4):
        y_copies = []
        for ch in range(NC):
            arrive(z_copies[ch])
            X[p - 1, ch * KC : (ch + 1) * KC] = total(Z.at[p - 1, ch])
            add_update(p, p - 1, ch * KC, KC)
            y_copies.append([
                send(
                    CT.at[p - 1, pl.ds(pl.multiple_of(KC * ch + YC * ring(y, k), 8), YC)],
                    Ry.at[p - 1, ch, k - 1], y_peer[k],
                )
                for k in order
            ])
        output_first(p - 1)
        if p == 1:
            u02 = spread(Uall, 1)
            d1 = forward(Dall, 0, d1)
        if p == 2:
            u13 = spread(Uall, 4)
            u03 = forward(Uall, 3, u03)

        h_copies = []
        for ch in range(NC):
            arrive(y_copies[ch])
            own = CT[p - 1, pl.ds(pl.multiple_of(KC * ch + YC * y, 8), YC), :]
            H[p - 1, ch, zh] = (own + Ry[p - 1, ch, 0]) + (Ry[p - 1, ch, 1] + Ry[p - 1, ch, 2])
            h_copies.append(share(H.at[p - 1, ch], zh, zh_peer))
        if p == 1:
            arrive(b_copies)
            u12 = spread(Uall, 2)
            ready_d(0, d1)
            ready_u(1, forward(Uall, 1, u02))
            add_update(2, 0, 0, KS)
            d2 = spread(Dall, 1)
        if p == 2:
            u23 = spread(Uall, 5)
            ready_d(1, d2)
            ready_u(3, u03)
            add_update(3, 0, 0, KS)
            ready_u(4, forward(Uall, 4, u13))
            add_update(3, 1, 0, KS)
            d3 = spread(Dall, 2)
        if p == 3:
            ready_d(2, d3)
        output_second(p - 1)

        a_copies = []
        for ch in range(NC):
            arrive(h_copies[ch])
            right = jnp.concatenate([bR[slot, p - 1, ch] for slot in range(8)], axis=1)
            CY[p - 1, ch, y] = right - total(H.at[p - 1, ch])
            a_copies.append(share(CY.at[p - 1, ch], y, y_peer))
        if p == 1:
            u12 = forward(Uall, 2, u12)
        if p == 2:
            u23 = forward(Uall, 5, u23)

        z_copies = []
        for ch in range(NC):
            arrive(a_copies[ch])
            high, low = split(CY[p - 1, ch].reshape(KC, 1024))
            Z[p, ch, zl] = dot3(high, low, Dh[p - 1], Dl[p - 1])
            z_copies.append(share(Z.at[p, ch], zl, zl_peer))
        if p == 1:
            u03 = spread(Uall, 3)
            ready_u(2, u12)
            d2 = forward(Dall, 1, d2)
        if p == 2:
            ready_u(5, u23)
            d3 = forward(Dall, 2, d3)
        output_third(p - 1)

    for ch in range(NC):
        arrive(z_copies[ch])
        X[3, ch * KC : (ch + 1) * KC] = total(Z.at[3, ch])
    output_first(3)
    output_second(3)
    output_third(3)
    for copy in started:
        copy.wait_send()
    for copy in stores:
        copy.wait()


def count_sends():
    return NC + 3 * NC + 7 + 9 * 4 + 4 * 3 * NC + 9 * 3 * NC + 4 * 4


def shards(factor, diag_inverse, right_side):
    sends = count_sends()
    solved = pl.pallas_call(
        kernel,
        out_shape=jax.ShapeDtypeStruct((4, 2, 4, 64, 256), F32),
        in_specs=[pl.BlockSpec(memory_space=pl.ANY)] * 3,
        out_specs=pl.BlockSpec(memory_space=pl.ANY),
        scratch_shapes=[
            pltpu.VMEM((3072, 128), F32),
            pltpu.VMEM((1024, 128), F32),
            pltpu.VMEM((4, 128, 512), F32),
            pltpu.VMEM((3, 512, 128), F32),
            pltpu.VMEM((8, 3, NC, YC, 128), F32),
            pltpu.VMEM((8, 3, NC, YC, 128), F32),
            pltpu.VMEM((6, 2, 4, 256, 128), F32),
            pltpu.VMEM((3, 2, 4, 128, 256), F32),
            pltpu.VMEM((6, 256, 1024), BF16),
            pltpu.VMEM((6, 256, 1024), BF16),
            pltpu.VMEM((3, 1024, 256), BF16),
            pltpu.VMEM((3, 1024, 256), BF16),
            pltpu.VMEM((2, NC, 4, KC, 256), F32),
            pltpu.VMEM((NC, 4, KC, 256), F32),
            pltpu.VMEM((NC, 3, KC, 256), F32),
            pltpu.VMEM((4, NC, 4, KC, 256), F32),
            pltpu.VMEM((3, KS, 1024), F32),
            pltpu.VMEM((3, NC, 3, YC, 1024), F32),
            pltpu.VMEM((3, NC, 4, YC, 1024), F32),
            pltpu.VMEM((3, NC, 4, YC, 1024), F32),
            pltpu.VMEM((4, KS, 256), F32),
            pltpu.VMEM((4, 2, 4, 64, 256), F32),
            pltpu.SemaphoreType.DMA((7,)),
            pltpu.SemaphoreType.DMA((sends,)),
            pltpu.SemaphoreType.DMA((sends,)),
        ],
        compiler_params=pltpu.CompilerParams(
            collective_id=0, has_side_effects=True, vmem_limit_bytes=56 * 1024 * 1024
        ),
        name="substitution",
    )(
        factor.reshape(4096, 128),
        diag_inverse.reshape(1024, 128),
        right_side.reshape(4, 128, 512),
    )
    pieces = solved.reshape(4, 512, 2, 128).transpose(0, 2, 3, 1)
    return pieces.reshape(8, 1, 128, 512)


def solution(mesh):
    return jax.shard_map(
        shards,
        mesh=mesh,
        in_specs=(
            P(None, "row", None, None, "col", None),
            P(None, None, "col", None, None, "row", None),
            P(None, "col", None, None),
        ),
        out_specs=P(None, "row", None, None),
        check_vma=False,
    )
```

```python
import functools

import jax
import jax.numpy as jnp
from jax import lax
from jax.experimental import pallas as pl
from jax.experimental.pallas import tpu as pltpu
from jax.sharding import PartitionSpec as P

F32 = jnp.float32
BF16 = jnp.bfloat16
MESH = pl.DeviceIdType.MESH
NC = 2
KS = 64
KC = KS // NC
YC = KC // 4
PAIRS = ((0, 1), (0, 2), (1, 2), (0, 3), (1, 3), (2, 3))
BLOCK = {pair: index for index, pair in enumerate(PAIRS)}


def split(value):
    high = value.astype(BF16)
    return high, (value - high.astype(F32)).astype(BF16)


def dot3(high, low, right_high, right_low):
    rows = high.shape[0]
    both = jnp.dot(
        jnp.concatenate([high, low], axis=0), right_high, preferred_element_type=F32
    )
    cross = jnp.dot(high, right_low, preferred_element_type=F32)
    return both[:rows] + (both[rows:] + cross)


def kernel(
    fac, dinv, rhs, out,
    facv, dinvv, bv, bT, bS, bR,
    Uall, Dall, Uh, Ul, Dh, Dl,
    P0, Rc, Rx, Z, CT, Ry, H, CY, X, OT,
    lsem, ssem, rsem, beyond,
):
    row = lax.axis_index("row")
    col = lax.axis_index("col")
    y, zh = row // 4, lax.rem(row, 4)
    x, zl, co = col // 8, lax.rem(col // 2, 4), lax.rem(col, 2)

    def dev(y_, zh_, x_, zl_, co_):
        return (y_ * 4 + zh_, (x_ * 4 + zl_) * 2 + co_)

    ring = lambda at, k: lax.rem(at + k, 4)
    core_peer = dev(y, zh, x, zl, 1 - co)
    x_peer = {k: dev(y, zh, ring(x, k), zl, co) for k in (1, 2, 3)}
    xc_peer = {k: dev(y, zh, ring(x, k), zl, 1 - co) for k in (1, 2, 3)}
    y_peer = {k: dev(ring(y, k), zh, x, zl, co) for k in (1, 2, 3)}
    zh_peer = {k: dev(y, ring(zh, k), x, zl, co) for k in (1, 2, 3)}
    zl_peer = {k: dev(y, zh, x, ring(zl, k), co) for k in (1, 2, 3)}
    order = (2, 1, 3)

    started = []

    def send(src, dst, peer):
        index = len(started)
        copy = pltpu.make_async_remote_copy(
            src_ref=src, dst_ref=dst, send_sem=ssem.at[index], recv_sem=rsem.at[index],
            device_id=peer, device_id_type=MESH,
        )
        copy.start()
        started.append(copy)
        return copy

    marks = []

    def drain():
        marks.append(len(started))
        if len(marks) > 3:
            for copy in started[0 if len(marks) == 4 else marks[-5] : marks[-4]]:
                copy.wait_send()

    def arrive(copies):
        for copy in copies:
            copy.wait_recv()

    loads = [
        pltpu.make_async_copy(dinv, dinvv, lsem.at[0]),
        pltpu.make_async_copy(rhs, bv, lsem.at[1]),
        pltpu.make_async_copy(fac.at[pl.ds(0, 3072)], facv, lsem.at[2]),
    ]
    for copy in loads:
        copy.start()
    barrier = pltpu.get_barrier_semaphore()
    greeted = [zh_peer[1], zh_peer[3]]
    for group in (zl_peer, x_peer, xc_peer, y_peer):
        greeted += [group[k] for k in order]
    greeted.append(core_peer)
    for peer in greeted:
        pl.semaphore_signal(barrier, inc=1, device_id=peer, device_id_type=MESH)

    loads[0].wait()
    loads[1].wait()
    d0 = jnp.concatenate(
        [dinvv[pl.ds(a, 128, stride=2), :] for a in range(2)], axis=1
    )
    d0h, d0l = split(d0)
    b0h, b0l = split(bv[0].T)
    for half in range(2):
        for quarter in range(4):
            at = 256 * half + 64 * quarter
            value = dot3(b0h[at : at + 64], b0l[at : at + 64], d0h, d0l)
            for ch in range(NC):
                P0[half, ch, quarter] = value[ch * KC : (ch + 1) * KC]

    loads[2].wait()
    for (q, p), block in BLOCK.items():
        Uall[block, 0, 0] = facv[pl.ds(1024 * q + p, 256, stride=4), :]
    for p in range(1, 4):
        for a in range(2):
            Dall[p - 1, 0, 0, :, a * 128 : (a + 1) * 128] = dinvv[
                pl.ds(256 * p + a, 128, stride=2), :
            ]

    pl.semaphore_wait(barrier, len(greeted))
    for k in (1, 3):
        pl.semaphore_signal(beyond, inc=1, device_id=zh_peer[k], device_id_type=MESH)

    near, far = (1, 3), (2,)
    spreads = {}

    def spread(buffer, block, steps):
        spreads.setdefault((buffer is Dall, block), []).extend(
            send(buffer.at[block, 0, 0], buffer.at[block, 0, k], x_peer[k]) for k in steps
        )

    def forward(buffer, block):
        arrive(spreads[(buffer is Dall, block)])
        return [send(buffer.at[block, 0], buffer.at[block, 1], core_peer)]

    def pass_on(block, k, index):
        arrive(spreads[(False, block)][index : index + 1])
        return send(Uall.at[block, 0, k], Uall.at[block, 1, k], core_peer)

    def ready_u(block, copies):
        arrive(copies)

        def body(slot, carry):
            high, low = split(Uall[block, slot // 4, lax.rem(slot, 4)])
            lanes = pl.ds(pl.multiple_of(slot * 128, 128), 128)
            Uh[block, :, lanes] = high
            Ul[block, :, lanes] = low
            return carry

        lax.fori_loop(0, 8, body, 0)

    def ready_d(block, copies):
        arrive(copies)

        def body(slot, carry):
            high, low = split(Dall[block, slot // 4, lax.rem(slot, 4)])
            rows = pl.ds(pl.multiple_of(slot * 128, 128), 128)
            Dh[block, rows, :] = high
            Dl[block, rows, :] = low
            return carry

        lax.fori_loop(0, 8, body, 0)

    def share(buffer, me, peers):
        return [send(buffer.at[me], buffer.at[me], peers[k]) for k in order]

    def total(buffer):
        return (buffer[0] + buffer[1]) + (buffer[2] + buffer[3])

    core_copies, x_copies, z_copies = {}, {}, {}

    def over_core(ch):
        core_copies[ch] = [send(P0.at[1 - co, ch], Rc.at[ch], core_peer)]

    def over_x(ch):
        arrive(core_copies[ch])
        P0[co, ch] = P0[co, ch] + Rc[ch]
        x_copies[ch] = [
            send(P0.at[co, ch, ring(x, k)], Rx.at[ch, k - 1], x_peer[k]) for k in order
        ]

    def over_z(ch):
        arrive(x_copies[ch])
        Z[0, ch, zl] = (P0[co, ch, x] + Rx[ch, 0]) + (Rx[ch, 1] + Rx[ch, 2])
        z_copies[ch] = share(Z.at[0, ch], zl, zl_peer)

    spread(Uall, 0, near)
    for ch in range(NC):
        over_core(ch)
    spread(Uall, 0, far)
    u01 = [send(Uall.at[0, 0, 0], Uall.at[0, 1, 0], core_peer)]
    for ch in range(NC):
        over_x(ch)
    u01 += [pass_on(0, k, index) for index, k in enumerate(near)]
    for ch in range(NC):
        over_z(ch)
    spread(Dall, 0, near)
    u01 += [pass_on(0, k, 2 + index) for index, k in enumerate(far)]

    for p in range(1, 4):
        bT[p - 1] = bv[p].T
    for dco in range(2):
        for dx in range(4):
            to_co = co if dco == 0 else 1 - co
            base = 256 * to_co + 64 * ring(x, dx) + YC * y
            for p in range(3):
                for ch in range(NC):
                    at = pl.multiple_of(base + KC * ch, 8)
                    piece = bT[p, pl.ds(at, YC), :]
                    if dco == 0 and dx == 0:
                        bR[0, p, ch] = piece
                    else:
                        bS[dco * 4 + dx, p, ch] = piece

    b_copies = []
    for dco in range(2):
        for dx in range(4):
            if dco or dx:
                peer = (x_peer[dx] if dco == 0 else core_peer if dx == 0 else xc_peer[dx])
                b_copies.append(send(bS.at[dco * 4 + dx], bR.at[dco * 4 + dx], peer))
    spread(Dall, 0, far)
    ready_u(0, u01)

    def add_update(p, q, first, count):
        block = BLOCK[(q, p)]
        high, low = split(X[q, pl.ds(first, count), :])
        for n in range(4):
            lanes = slice(256 * n, 256 * (n + 1))
            value = dot3(high, low, Uh[block, :, lanes], Ul[block, :, lanes])
            if q > 0:
                value = value + CT[p - 1, pl.ds(first, count), lanes]
            CT[p - 1, pl.ds(first, count), lanes] = value

    out_first = {}
    out_second = {}
    stores = []

    def output_first(p):
        for a in range(2):
            OT[p, co, x, a] = X[p, :, a * 128 : (a + 1) * 128]
        out_first[p] = [
            send(OT.at[p, co, x], OT.at[p, co, x], x_peer[k]) for k in order
        ]

    def output_second(p):
        arrive(out_first[p])
        out_second[p] = [send(OT.at[p, co], OT.at[p, co], core_peer)]

    def output_third(p):
        arrive(out_second.get(p, []))
        for a in range(2):
            copy = pltpu.make_async_copy(
                OT.at[p, :, :, a], out.at[p, a], lsem.at[3 + 2 * p + a]
            )
            copy.start()
            stores.append(copy)

    pending = {}
    for p in range(1, 4):
        y_copies = []
        for ch in range(NC):
            arrive(z_copies[ch])
            X[p - 1, ch * KC : (ch + 1) * KC] = total(Z.at[p - 1, ch])
            add_update(p, p - 1, ch * KC, KC)
            y_copies.append([
                send(
                    CT.at[p - 1, pl.ds(pl.multiple_of(KC * ch + YC * ring(y, k), 8), YC)],
                    Ry.at[p - 1, ch, k - 1], y_peer[k],
                )
                for k in order
            ])
        output_first(p - 1)
        if p == 1:
            spread(Uall, 1, near)
            d1 = forward(Dall, 0)
        if p == 2:
            spread(Uall, 3, far)
            d2 = forward(Dall, 1)
        if p == 3:
            d3 = forward(Dall, 2)

        drain()
        if p == 1:
            pl.semaphore_wait(beyond, 2)
        h_copies = []
        for ch in range(NC):
            arrive(y_copies[ch])
            own = CT[p - 1, pl.ds(pl.multiple_of(KC * ch + YC * y, 8), YC), :]
            H[p - 1, ch, zh] = (own + Ry[p - 1, ch, 0]) + (Ry[p - 1, ch, 1] + Ry[p - 1, ch, 2])
            h_copies.append(share(H.at[p - 1, ch], zh, zh_peer))
        output_second(p - 1)
        if p == 1:
            spread(Uall, 1, far)
            spread(Uall, 2, near)
            arrive(b_copies)
            ready_d(0, d1)
            spread(Uall, 2, far)
            u02 = forward(Uall, 1)
        if p == 2:
            spread(Uall, 4, near)
            spread(Uall, 4, far)
            ready_d(1, d2)
            spread(Uall, 5, near)
            u03 = forward(Uall, 3)
        if p == 3:
            ready_d(2, d3)

        drain()
        a_copies = []
        for ch in range(NC):
            arrive(h_copies[ch])
            right = jnp.concatenate([bR[slot, p - 1, ch] for slot in range(8)], axis=1)
            CY[p - 1, ch, y] = right - total(H.at[p - 1, ch])
            a_copies.append(share(CY.at[p - 1, ch], y, y_peer))
        if p == 1:
            spread(Dall, 1, near)
            u12 = forward(Uall, 2)
        if p == 2:
            spread(Uall, 5, far)
            u13 = forward(Uall, 4)

        drain()
        z_copies = []
        for ch in range(NC):
            arrive(a_copies[ch])
            high, low = split(CY[p - 1, ch].reshape(KC, 1024))
            Z[p, ch, zl] = dot3(high, low, Dh[p - 1], Dl[p - 1])
            z_copies.append(share(Z.at[p, ch], zl, zl_peer))
        if p == 1:
            spread(Dall, 1, far)
            ready_u(1, u02)
            add_update(2, 0, 0, KS)
            spread(Uall, 3, near)
            ready_u(2, u12)
        if p == 2:
            spread(Dall, 2, near)
            u23 = forward(Uall, 5)
            ready_u(3, u03)
            add_update(3, 0, 0, KS)
            ready_u(4, u13)
            add_update(3, 1, 0, KS)
            spread(Dall, 2, far)
            ready_u(5, u23)
        output_third(p - 1)
        drain()

    last_x, last_core = [], []
    for ch in range(NC):
        rows = slice(ch * KC, (ch + 1) * KC)
        arrive(z_copies[ch])
        value = total(Z.at[3, ch])
        for a in range(2):
            OT[3, co, x, a, rows] = value[:, a * 128 : (a + 1) * 128]
        piece = OT.at[3, co, x, :, pl.ds(ch * KC, KC)]
        last_x.append([send(piece, piece, x_peer[k]) for k in order])
    for ch in range(NC):
        arrive(last_x[ch])
        piece = OT.at[3, co, :, :, pl.ds(ch * KC, KC)]
        last_core.append([send(piece, piece, core_peer)])
    for ch in range(NC):
        arrive(last_core[ch])
    output_third(3)
    for copy in started[marks[-4] :]:
        copy.wait_send()
    for copy in stores:
        copy.wait()


def count_sends():
    return NC + 3 * NC + 7 + 9 * 4 + 3 + 4 * 3 * NC + 9 * 3 * NC + 3 * 4 + 4 * NC


def shards(factor, diag_inverse, right_side):
    sends = count_sends()
    solved = pl.pallas_call(
        kernel,
        out_shape=jax.ShapeDtypeStruct((4, 2, 2, 4, 64, 128), F32),
        in_specs=[pl.BlockSpec(memory_space=pl.ANY)] * 3,
        out_specs=pl.BlockSpec(memory_space=pl.ANY),
        scratch_shapes=[
            pltpu.VMEM((3072, 128), F32),
            pltpu.VMEM((1024, 128), F32),
            pltpu.VMEM((4, 128, 512), F32),
            pltpu.VMEM((3, 512, 128), F32),
            pltpu.VMEM((8, 3, NC, YC, 128), F32),
            pltpu.VMEM((8, 3, NC, YC, 128), F32),
            pltpu.VMEM((6, 2, 4, 256, 128), F32),
            pltpu.VMEM((3, 2, 4, 128, 256), F32),
            pltpu.VMEM((6, 256, 1024), BF16),
            pltpu.VMEM((6, 256, 1024), BF16),
            pltpu.VMEM((3, 1024, 256), BF16),
            pltpu.VMEM((3, 1024, 256), BF16),
            pltpu.VMEM((2, NC, 4, KC, 256), F32),
            pltpu.VMEM((NC, 4, KC, 256), F32),
            pltpu.VMEM((NC, 3, KC, 256), F32),
            pltpu.VMEM((4, NC, 4, KC, 256), F32),
            pltpu.VMEM((3, KS, 1024), F32),
            pltpu.VMEM((3, NC, 3, YC, 1024), F32),
            pltpu.VMEM((3, NC, 4, YC, 1024), F32),
            pltpu.VMEM((3, NC, 4, YC, 1024), F32),
            pltpu.VMEM((4, KS, 256), F32),
            pltpu.VMEM((4, 2, 4, 2, 64, 128), F32),
            pltpu.SemaphoreType.DMA((11,)),
            pltpu.SemaphoreType.DMA((sends,)),
            pltpu.SemaphoreType.DMA((sends,)),
            pltpu.SemaphoreType.REGULAR,
        ],
        compiler_params=pltpu.CompilerParams(
            collective_id=0, has_side_effects=True, vmem_limit_bytes=56 * 1024 * 1024
        ),
        name="substitution",
    )(
        factor.reshape(4096, 128),
        diag_inverse.reshape(1024, 128),
        right_side.reshape(4, 128, 512),
    )
    pieces = solved.reshape(8, 512, 128).transpose(0, 2, 1)
    return pieces.reshape(8, 1, 128, 512)


def solution(mesh):
    return jax.shard_map(
        shards,
        mesh=mesh,
        in_specs=(
            P(None, "row", None, None, "col", None),
            P(None, None, "col", None, None, "row", None),
            P(None, "col", None, None),
        ),
        out_specs=P(None, "row", None, None),
        check_vma=False,
    )
```

```python
import functools

import jax
import jax.numpy as jnp
from jax import lax
from jax.experimental import pallas as pl
from jax.experimental.pallas import tpu as pltpu
from jax.sharding import PartitionSpec as P

F32 = jnp.float32
BF16 = jnp.bfloat16
MESH = pl.DeviceIdType.MESH
NC = 2
KS = 64
KC = KS // NC
YC = KC // 4
PAIRS = ((0, 1), (0, 2), (1, 2), (0, 3), (1, 3), (2, 3))
BLOCK = {pair: index for index, pair in enumerate(PAIRS)}


def split(value):
    high = value.astype(BF16)
    return high, (value - high.astype(F32)).astype(BF16)


def dot3(high, low, right_high, right_low):
    rows = high.shape[0]
    both = jnp.dot(
        jnp.concatenate([high, low], axis=0), right_high, preferred_element_type=F32
    )
    cross = jnp.dot(high, right_low, preferred_element_type=F32)
    return both[:rows] + (both[rows:] + cross)


def kernel(
    fac, dinv, rhs, out,
    facv, dinvv, bv, bT, bS, bR,
    Uall, Dall, Uh, Ul, Dh, Dl,
    P0, Rc, Rx, Z, CT, Ry, H, CY, X, OT,
    lsem, ssem, rsem, beyond,
):
    row = lax.axis_index("row")
    col = lax.axis_index("col")
    y, zh = row // 4, lax.rem(row, 4)
    x, zl, co = col // 8, lax.rem(col // 2, 4), lax.rem(col, 2)

    def dev(y_, zh_, x_, zl_, co_):
        return (y_ * 4 + zh_, (x_ * 4 + zl_) * 2 + co_)

    ring = lambda at, k: lax.rem(at + k, 4)
    core_peer = dev(y, zh, x, zl, 1 - co)
    x_peer = {k: dev(y, zh, ring(x, k), zl, co) for k in (1, 2, 3)}
    xc_peer = {k: dev(y, zh, ring(x, k), zl, 1 - co) for k in (1, 2, 3)}
    y_peer = {k: dev(ring(y, k), zh, x, zl, co) for k in (1, 2, 3)}
    zh_peer = {k: dev(y, ring(zh, k), x, zl, co) for k in (1, 2, 3)}
    zl_peer = {k: dev(y, zh, x, ring(zl, k), co) for k in (1, 2, 3)}
    order = (2, 1, 3)

    started = []

    def send(src, dst, peer):
        index = len(started)
        copy = pltpu.make_async_remote_copy(
            src_ref=src, dst_ref=dst, send_sem=ssem.at[index], recv_sem=rsem.at[index],
            device_id=peer, device_id_type=MESH,
        )
        copy.start()
        started.append(copy)
        return copy

    marks = []

    def drain():
        marks.append(len(started))
        if len(marks) > 3:
            for copy in started[0 if len(marks) == 4 else marks[-5] : marks[-4]]:
                copy.wait_send()

    def arrive(copies):
        for copy in copies:
            copy.wait_recv()

    loads = [
        pltpu.make_async_copy(dinv, dinvv, lsem.at[0]),
        pltpu.make_async_copy(rhs, bv, lsem.at[1]),
        pltpu.make_async_copy(fac.at[pl.ds(0, 3072)], facv, lsem.at[2]),
    ]
    for copy in loads:
        copy.start()
    barrier = pltpu.get_barrier_semaphore()
    greeted = [zh_peer[1], zh_peer[3]]
    for group in (zl_peer, x_peer, xc_peer, y_peer):
        greeted += [group[k] for k in order]
    greeted.append(core_peer)
    for peer in greeted:
        pl.semaphore_signal(barrier, inc=1, device_id=peer, device_id_type=MESH)

    loads[0].wait()
    loads[1].wait()
    d0 = jnp.concatenate(
        [dinvv[pl.ds(a, 128, stride=2), :] for a in range(2)], axis=1
    )
    d0h, d0l = split(d0)
    b0h, b0l = split(bv[0].T)
    for half in range(2):
        for quarter in range(4):
            at = 256 * half + 64 * quarter
            value = dot3(b0h[at : at + 64], b0l[at : at + 64], d0h, d0l)
            for ch in range(NC):
                P0[half, ch, quarter] = value[ch * KC : (ch + 1) * KC]

    loads[2].wait()
    for (q, p), block in BLOCK.items():
        Uall[block, 0, 0] = facv[pl.ds(1024 * q + p, 256, stride=4), :]
    for p in range(1, 4):
        for a in range(2):
            Dall[p - 1, 0, 0, :, a * 128 : (a + 1) * 128] = dinvv[
                pl.ds(256 * p + a, 128, stride=2), :
            ]

    pl.semaphore_wait(barrier, len(greeted))
    for k in (1, 3):
        pl.semaphore_signal(beyond, inc=1, device_id=zh_peer[k], device_id_type=MESH)

    near, far = (1, 3), (2,)
    spreads = {}

    def spread(buffer, block, steps):
        spreads.setdefault((buffer is Dall, block), []).extend(
            send(buffer.at[block, 0, 0], buffer.at[block, 0, k], x_peer[k]) for k in steps
        )

    def forward(buffer, block):
        arrive(spreads[(buffer is Dall, block)])
        return [send(buffer.at[block, 0], buffer.at[block, 1], core_peer)]

    def pass_on(block, k, index):
        arrive(spreads[(False, block)][index : index + 1])
        return send(Uall.at[block, 0, k], Uall.at[block, 1, k], core_peer)

    def ready_u(block, copies):
        arrive(copies)

        def body(slot, carry):
            high, low = split(Uall[block, slot // 4, lax.rem(slot, 4)])
            lanes = pl.ds(pl.multiple_of(slot * 128, 128), 128)
            Uh[block, :, lanes] = high
            Ul[block, :, lanes] = low
            return carry

        lax.fori_loop(0, 8, body, 0)

    def ready_d(block, copies):
        arrive(copies)

        def body(slot, carry):
            high, low = split(Dall[block, slot // 4, lax.rem(slot, 4)])
            rows = pl.ds(pl.multiple_of(slot * 128, 128), 128)
            Dh[block, rows, :] = high
            Dl[block, rows, :] = low
            return carry

        lax.fori_loop(0, 8, body, 0)

    def share(buffer, me, peers):
        return [send(buffer.at[me], buffer.at[me], peers[k]) for k in order]

    def total(buffer):
        return (buffer[0] + buffer[1]) + (buffer[2] + buffer[3])

    core_copies, x_copies, z_copies = {}, {}, {}

    def over_core(ch):
        core_copies[ch] = [send(P0.at[1 - co, ch], Rc.at[ch], core_peer)]

    def over_x(ch):
        arrive(core_copies[ch])
        P0[co, ch] = P0[co, ch] + Rc[ch]
        x_copies[ch] = [
            send(P0.at[co, ch, ring(x, k)], Rx.at[ch, k - 1], x_peer[k]) for k in order
        ]

    def over_z(ch):
        arrive(x_copies[ch])
        Z[0, ch, zl] = (P0[co, ch, x] + Rx[ch, 0]) + (Rx[ch, 1] + Rx[ch, 2])
        z_copies[ch] = share(Z.at[0, ch], zl, zl_peer)

    spread(Uall, 0, near)
    for ch in range(NC):
        over_core(ch)
    u01 = [send(Uall.at[0, 0, 0], Uall.at[0, 1, 0], core_peer)]
    for ch in range(NC):
        over_x(ch)
    spread(Uall, 0, far)
    u01 += [pass_on(0, k, index) for index, k in enumerate(near)]
    for ch in range(NC):
        over_z(ch)
    spread(Dall, 0, near)
    u01 += [pass_on(0, k, 2 + index) for index, k in enumerate(far)]

    for p in range(1, 4):
        bT[p - 1] = bv[p].T
    for dco in range(2):
        for dx in range(4):
            to_co = co if dco == 0 else 1 - co
            base = 256 * to_co + 64 * ring(x, dx) + YC * y
            for p in range(3):
                for ch in range(NC):
                    at = pl.multiple_of(base + KC * ch, 8)
                    piece = bT[p, pl.ds(at, YC), :]
                    if dco == 0 and dx == 0:
                        bR[0, p, ch] = piece
                    else:
                        bS[dco * 4 + dx, p, ch] = piece

    b_copies = []
    for dco in range(2):
        for dx in range(4):
            if dco or dx:
                peer = (x_peer[dx] if dco == 0 else core_peer if dx == 0 else xc_peer[dx])
                b_copies.append(send(bS.at[dco * 4 + dx], bR.at[dco * 4 + dx], peer))
    spread(Dall, 0, far)
    ready_u(0, u01)

    def add_update(p, q, first, count):
        block = BLOCK[(q, p)]
        high, low = split(X[q, pl.ds(first, count), :])
        for n in range(4):
            lanes = slice(256 * n, 256 * (n + 1))
            value = dot3(high, low, Uh[block, :, lanes], Ul[block, :, lanes])
            if q > 0:
                value = value + CT[p - 1, pl.ds(first, count), lanes]
            CT[p - 1, pl.ds(first, count), lanes] = value

    out_first = {}
    out_second = {}
    stores = []

    def output_first(p):
        for a in range(2):
            OT[p, co, x, a] = X[p, :, a * 128 : (a + 1) * 128]
        out_first[p] = [
            send(OT.at[p, co, x], OT.at[p, co, x], x_peer[k]) for k in order
        ]

    def output_second(p):
        arrive(out_first[p])
        out_second[p] = [send(OT.at[p, co], OT.at[p, co], core_peer)]

    def output_third(p):
        arrive(out_second.get(p, []))
        for a in range(2):
            copy = pltpu.make_async_copy(
                OT.at[p, :, :, a], out.at[p, a], lsem.at[3 + 2 * p + a]
            )
            copy.start()
            stores.append(copy)

    pending = {}
    for p in range(1, 4):
        y_copies = []
        for ch in range(NC):
            arrive(z_copies[ch])
            X[p - 1, ch * KC : (ch + 1) * KC] = total(Z.at[p - 1, ch])
            add_update(p, p - 1, ch * KC, KC)
            y_copies.append([
                send(
                    CT.at[p - 1, pl.ds(pl.multiple_of(KC * ch + YC * ring(y, k), 8), YC)],
                    Ry.at[p - 1, ch, k - 1], y_peer[k],
                )
                for k in order
            ])
        output_first(p - 1)
        if p == 1:
            spread(Uall, 1, near)
            d1 = forward(Dall, 0)
        if p == 2:
            spread(Uall, 3, far)
            d2 = forward(Dall, 1)
        if p == 3:
            d3 = forward(Dall, 2)

        drain()
        if p == 1:
            pl.semaphore_wait(beyond, 2)
        h_copies = []
        for ch in range(NC):
            arrive(y_copies[ch])
            own = CT[p - 1, pl.ds(pl.multiple_of(KC * ch + YC * y, 8), YC), :]
            H[p - 1, ch, zh] = (own + Ry[p - 1, ch, 0]) + (Ry[p - 1, ch, 1] + Ry[p - 1, ch, 2])
            h_copies.append(share(H.at[p - 1, ch], zh, zh_peer))
        output_second(p - 1)
        if p == 1:
            spread(Uall, 1, far)
            spread(Uall, 2, near)
            arrive(b_copies)
            ready_d(0, d1)
            spread(Uall, 2, far)
            u02 = forward(Uall, 1)
        if p == 2:
            spread(Uall, 4, near)
            spread(Uall, 4, far)
            ready_d(1, d2)
            spread(Uall, 5, near)
            u03 = forward(Uall, 3)
        if p == 3:
            ready_d(2, d3)

        drain()
        a_copies = []
        for ch in range(NC):
            arrive(h_copies[ch])
            right = jnp.concatenate([bR[slot, p - 1, ch] for slot in range(8)], axis=1)
            CY[p - 1, ch, y] = right - total(H.at[p - 1, ch])
            a_copies.append(share(CY.at[p - 1, ch], y, y_peer))
        if p == 1:
            spread(Dall, 1, near)
            u12 = forward(Uall, 2)
        if p == 2:
            spread(Uall, 5, far)
            u13 = forward(Uall, 4)

        drain()
        z_copies = []
        for ch in range(NC):
            arrive(a_copies[ch])
            high, low = split(CY[p - 1, ch].reshape(KC, 1024))
            Z[p, ch, zl] = dot3(high, low, Dh[p - 1], Dl[p - 1])
            z_copies.append(share(Z.at[p, ch], zl, zl_peer))
        if p == 1:
            spread(Dall, 1, far)
            ready_u(1, u02)
            add_update(2, 0, 0, KS)
            spread(Uall, 3, near)
            ready_u(2, u12)
        if p == 2:
            spread(Dall, 2, near)
            u23 = forward(Uall, 5)
            ready_u(3, u03)
            add_update(3, 0, 0, KS)
            ready_u(4, u13)
            add_update(3, 1, 0, KS)
            spread(Dall, 2, far)
            ready_u(5, u23)
        output_third(p - 1)
        drain()

    last_x, last_core = [], []
    for ch in range(NC):
        rows = slice(ch * KC, (ch + 1) * KC)
        arrive(z_copies[ch])
        value = total(Z.at[3, ch])
        for a in range(2):
            OT[3, co, x, a, rows] = value[:, a * 128 : (a + 1) * 128]
        piece = OT.at[3, co, x, :, pl.ds(ch * KC, KC)]
        last_x.append([send(piece, piece, x_peer[k]) for k in order])
    for ch in range(NC):
        arrive(last_x[ch])
        piece = OT.at[3, co, :, :, pl.ds(ch * KC, KC)]
        last_core.append([send(piece, piece, core_peer)])
    for ch in range(NC):
        arrive(last_core[ch])
    output_third(3)
    for copy in started[marks[-4] :]:
        copy.wait_send()
    for copy in stores:
        copy.wait()


def count_sends():
    return NC + 3 * NC + 7 + 9 * 4 + 3 + 4 * 3 * NC + 9 * 3 * NC + 3 * 4 + 4 * NC


def shards(factor, diag_inverse, right_side):
    sends = count_sends()
    solved = pl.pallas_call(
        kernel,
        out_shape=pltpu.VMEM((4, 2, 2, 4, 64, 128), F32),
        in_specs=[pl.BlockSpec(memory_space=pl.ANY)] * 3,
        out_specs=pl.BlockSpec(memory_space=pltpu.VMEM),
        scratch_shapes=[
            pltpu.VMEM((3072, 128), F32),
            pltpu.VMEM((1024, 128), F32),
            pltpu.VMEM((4, 128, 512), F32),
            pltpu.VMEM((3, 512, 128), F32),
            pltpu.VMEM((8, 3, NC, YC, 128), F32),
            pltpu.VMEM((8, 3, NC, YC, 128), F32),
            pltpu.VMEM((6, 2, 4, 256, 128), F32),
            pltpu.VMEM((3, 2, 4, 128, 256), F32),
            pltpu.VMEM((6, 256, 1024), BF16),
            pltpu.VMEM((6, 256, 1024), BF16),
            pltpu.VMEM((3, 1024, 256), BF16),
            pltpu.VMEM((3, 1024, 256), BF16),
            pltpu.VMEM((2, NC, 4, KC, 256), F32),
            pltpu.VMEM((NC, 4, KC, 256), F32),
            pltpu.VMEM((NC, 3, KC, 256), F32),
            pltpu.VMEM((4, NC, 4, KC, 256), F32),
            pltpu.VMEM((3, KS, 1024), F32),
            pltpu.VMEM((3, NC, 3, YC, 1024), F32),
            pltpu.VMEM((3, NC, 4, YC, 1024), F32),
            pltpu.VMEM((3, NC, 4, YC, 1024), F32),
            pltpu.VMEM((4, KS, 256), F32),
            pltpu.VMEM((4, 2, 4, 2, 64, 128), F32),
            pltpu.SemaphoreType.DMA((11,)),
            pltpu.SemaphoreType.DMA((sends,)),
            pltpu.SemaphoreType.DMA((sends,)),
            pltpu.SemaphoreType.REGULAR,
        ],
        compiler_params=pltpu.CompilerParams(
            collective_id=0, has_side_effects=True, vmem_limit_bytes=56 * 1024 * 1024
        ),
        name="substitution",
    )(
        factor.reshape(4096, 128),
        diag_inverse.reshape(1024, 128),
        right_side.reshape(4, 128, 512),
    )
    pieces = solved.reshape(8, 512, 128).transpose(0, 2, 1)
    return pieces.reshape(8, 1, 128, 512)


def solution(mesh):
    return jax.shard_map(
        shards,
        mesh=mesh,
        in_specs=(
            P(None, "row", None, None, "col", None),
            P(None, None, "col", None, None, "row", None),
            P(None, "col", None, None),
        ),
        out_specs=P(None, "row", None, None),
        check_vma=False,
    )
```

```python
import functools

import jax
import jax.numpy as jnp
from jax import lax
from jax.experimental import pallas as pl
from jax.experimental.pallas import tpu as pltpu
from jax.sharding import PartitionSpec as P

F32 = jnp.float32
BF16 = jnp.bfloat16
MESH = pl.DeviceIdType.MESH
NC = 2
KS = 64
KC = KS // NC
YC = KC // 4
PAIRS = ((0, 1), (0, 2), (1, 2), (0, 3), (1, 3), (2, 3))
BLOCK = {pair: index for index, pair in enumerate(PAIRS)}


def split(value):
    high = value.astype(BF16)
    return high, (value - high.astype(F32)).astype(BF16)


def dot3(high, low, right_high, right_low):
    rows = high.shape[0]
    both = jnp.dot(
        jnp.concatenate([high, low], axis=0), right_high, preferred_element_type=F32
    )
    cross = jnp.dot(high, right_low, preferred_element_type=F32)
    return both[:rows] + (both[rows:] + cross)


def kernel(
    fac, dinv, rhs, out,
    facv, dinvv, bv, bT, bS, bR,
    Uall, Dall, Uh, Ul, Dh, Dl,
    P0, Rc, Rx, Z, CT, Ry, H, CY, X, OT,
    lsem, ssem, rsem, beyond,
):
    row = lax.axis_index("row")
    col = lax.axis_index("col")
    y, zh = row // 4, lax.rem(row, 4)
    x, zl, co = col // 8, lax.rem(col // 2, 4), lax.rem(col, 2)

    def dev(y_, zh_, x_, zl_, co_):
        return (y_ * 4 + zh_, (x_ * 4 + zl_) * 2 + co_)

    ring = lambda at, k: lax.rem(at + k, 4)
    core_peer = dev(y, zh, x, zl, 1 - co)
    x_peer = {k: dev(y, zh, ring(x, k), zl, co) for k in (1, 2, 3)}
    xc_peer = {k: dev(y, zh, ring(x, k), zl, 1 - co) for k in (1, 2, 3)}
    y_peer = {k: dev(ring(y, k), zh, x, zl, co) for k in (1, 2, 3)}
    zh_peer = {k: dev(y, ring(zh, k), x, zl, co) for k in (1, 2, 3)}
    zl_peer = {k: dev(y, zh, x, ring(zl, k), co) for k in (1, 2, 3)}
    order = (2, 1, 3)

    started = []

    def send(src, dst, peer):
        index = len(started)
        copy = pltpu.make_async_remote_copy(
            src_ref=src, dst_ref=dst, send_sem=ssem.at[index], recv_sem=rsem.at[index],
            device_id=peer, device_id_type=MESH,
        )
        copy.start()
        started.append(copy)
        return copy

    marks = []

    def drain():
        marks.append(len(started))
        if len(marks) > 3:
            for copy in started[0 if len(marks) == 4 else marks[-5] : marks[-4]]:
                copy.wait_send()

    def arrive(copies):
        for copy in copies:
            copy.wait_recv()

    loads = [
        pltpu.make_async_copy(dinv, dinvv, lsem.at[0]),
        pltpu.make_async_copy(rhs, bv, lsem.at[1]),
        pltpu.make_async_copy(fac.at[pl.ds(0, 3072)], facv, lsem.at[2]),
    ]
    for copy in loads:
        copy.start()
    barrier = pltpu.get_barrier_semaphore()
    greeted = [zh_peer[1], zh_peer[3]]
    for group in (zl_peer, x_peer, xc_peer, y_peer):
        greeted += [group[k] for k in order]
    greeted.append(core_peer)
    for peer in greeted:
        pl.semaphore_signal(barrier, inc=1, device_id=peer, device_id_type=MESH)

    loads[0].wait()
    loads[1].wait()
    d0 = jnp.concatenate(
        [dinvv[pl.ds(a, 128, stride=2), :] for a in range(2)], axis=1
    )
    d0h, d0l = split(d0)
    b0h, b0l = split(bv[0].T)
    for half in range(2):
        for quarter in range(4):
            at = 256 * half + 64 * quarter
            value = dot3(b0h[at : at + 64], b0l[at : at + 64], d0h, d0l)
            for ch in range(NC):
                P0[half, ch, quarter] = value[ch * KC : (ch + 1) * KC]

    loads[2].wait()
    for (q, p), block in BLOCK.items():
        Uall[block, 0, 0] = facv[pl.ds(1024 * q + p, 256, stride=4), :]
    for p in range(1, 4):
        for a in range(2):
            Dall[p - 1, 0, 0, :, a * 128 : (a + 1) * 128] = dinvv[
                pl.ds(256 * p + a, 128, stride=2), :
            ]

    pl.semaphore_wait(barrier, len(greeted))
    for k in (1, 3):
        pl.semaphore_signal(beyond, inc=1, device_id=zh_peer[k], device_id_type=MESH)

    near, far = (1, 3), (2,)
    spreads = {}

    def spread(buffer, block, steps):
        spreads.setdefault((buffer is Dall, block), []).extend(
            send(buffer.at[block, 0, 0], buffer.at[block, 0, k], x_peer[k]) for k in steps
        )

    def relay(buffer, block):
        copies = spreads[(buffer is Dall, block)]
        arrive(copies)
        half = buffer.shape[3] // 2
        for k in near:
            rows = pl.ds(0 if k == 1 else half, half)
            copies.append(
                send(buffer.at[block, 0, k, rows], buffer.at[block, 0, 2, rows], x_peer[k])
            )

    def forward(buffer, block):
        copies = spreads[(buffer is Dall, block)]
        arrive(copies[2:] if len(copies) > 3 else copies)
        return [send(buffer.at[block, 0], buffer.at[block, 1], core_peer)]

    def pass_on(block, k, index):
        arrive(spreads[(False, block)][index : index + 1])
        return send(Uall.at[block, 0, k], Uall.at[block, 1, k], core_peer)

    def ready_u(block, copies):
        arrive(copies)

        def body(slot, carry):
            high, low = split(Uall[block, slot // 4, lax.rem(slot, 4)])
            lanes = pl.ds(pl.multiple_of(slot * 128, 128), 128)
            Uh[block, :, lanes] = high
            Ul[block, :, lanes] = low
            return carry

        lax.fori_loop(0, 8, body, 0)

    def ready_d(block, copies):
        arrive(copies)

        def body(slot, carry):
            high, low = split(Dall[block, slot // 4, lax.rem(slot, 4)])
            rows = pl.ds(pl.multiple_of(slot * 128, 128), 128)
            Dh[block, rows, :] = high
            Dl[block, rows, :] = low
            return carry

        lax.fori_loop(0, 8, body, 0)

    def share(buffer, me, peers):
        return [send(buffer.at[me], buffer.at[me], peers[k]) for k in order]

    def total(buffer):
        return (buffer[0] + buffer[1]) + (buffer[2] + buffer[3])

    core_copies, x_copies, z_copies = {}, {}, {}

    def over_core(ch):
        core_copies[ch] = [send(P0.at[1 - co, ch], Rc.at[ch], core_peer)]

    def over_x(ch):
        arrive(core_copies[ch])
        P0[co, ch] = P0[co, ch] + Rc[ch]
        x_copies[ch] = [
            send(P0.at[co, ch, ring(x, k)], Rx.at[ch, k - 1], x_peer[k]) for k in order
        ]

    def over_z(ch):
        arrive(x_copies[ch])
        Z[0, ch, zl] = (P0[co, ch, x] + Rx[ch, 0]) + (Rx[ch, 1] + Rx[ch, 2])
        z_copies[ch] = share(Z.at[0, ch], zl, zl_peer)

    spread(Uall, 0, near)
    for ch in range(NC):
        over_core(ch)
    u01 = [send(Uall.at[0, 0, 0], Uall.at[0, 1, 0], core_peer)]
    for ch in range(NC):
        over_x(ch)
    spread(Uall, 0, far)
    u01 += [pass_on(0, k, index) for index, k in enumerate(near)]
    for ch in range(NC):
        over_z(ch)
    spread(Dall, 0, near)
    u01 += [pass_on(0, k, 2 + index) for index, k in enumerate(far)]

    for p in range(1, 4):
        bT[p - 1] = bv[p].T
    for dco in range(2):
        for dx in range(4):
            to_co = co if dco == 0 else 1 - co
            base = 256 * to_co + 64 * ring(x, dx) + YC * y
            for p in range(3):
                for ch in range(NC):
                    at = pl.multiple_of(base + KC * ch, 8)
                    piece = bT[p, pl.ds(at, YC), :]
                    if dco == 0 and dx == 0:
                        bR[0, p, ch] = piece
                    else:
                        bS[dco * 4 + dx, p, ch] = piece

    b_copies = []
    for dco in range(2):
        for dx in range(4):
            if dco or dx:
                peer = (x_peer[dx] if dco == 0 else core_peer if dx == 0 else xc_peer[dx])
                b_copies.append(send(bS.at[dco * 4 + dx], bR.at[dco * 4 + dx], peer))
    ready_u(0, u01)

    def add_update(p, q, first, count):
        block = BLOCK[(q, p)]
        high, low = split(X[q, pl.ds(first, count), :])
        for n in range(4):
            lanes = slice(256 * n, 256 * (n + 1))
            value = dot3(high, low, Uh[block, :, lanes], Ul[block, :, lanes])
            if q > 0:
                value = value + CT[p - 1, pl.ds(first, count), lanes]
            CT[p - 1, pl.ds(first, count), lanes] = value

    out_first = {}
    out_second = {}
    stores = []

    def output_first(p):
        for a in range(2):
            OT[p, co, x, a] = X[p, :, a * 128 : (a + 1) * 128]
        out_first[p] = [
            send(OT.at[p, co, x], OT.at[p, co, x], x_peer[k]) for k in order
        ]

    def output_second(p):
        arrive(out_first[p])
        out_second[p] = [send(OT.at[p, co], OT.at[p, co], core_peer)]

    def output_third(p):
        arrive(out_second.get(p, []))
        for a in range(2):
            copy = pltpu.make_async_copy(
                OT.at[p, :, :, a], out.at[p, a], lsem.at[3 + 2 * p + a]
            )
            copy.start()
            stores.append(copy)

    pending = {}
    for p in range(1, 4):
        y_copies = []
        for ch in range(NC):
            arrive(z_copies[ch])
            X[p - 1, ch * KC : (ch + 1) * KC] = total(Z.at[p - 1, ch])
            add_update(p, p - 1, ch * KC, KC)
            y_copies.append([
                send(
                    CT.at[p - 1, pl.ds(pl.multiple_of(KC * ch + YC * ring(y, k), 8), YC)],
                    Ry.at[p - 1, ch, k - 1], y_peer[k],
                )
                for k in order
            ])
        output_first(p - 1)
        if p == 1:
            spread(Uall, 1, near)
            relay(Dall, 0)
        if p == 2:
            spread(Uall, 3, far)
            d2 = forward(Dall, 1)
        if p == 3:
            d3 = forward(Dall, 2)

        drain()
        if p == 1:
            pl.semaphore_wait(beyond, 2)
        h_copies = []
        for ch in range(NC):
            arrive(y_copies[ch])
            own = CT[p - 1, pl.ds(pl.multiple_of(KC * ch + YC * y, 8), YC), :]
            H[p - 1, ch, zh] = (own + Ry[p - 1, ch, 0]) + (Ry[p - 1, ch, 1] + Ry[p - 1, ch, 2])
            h_copies.append(share(H.at[p - 1, ch], zh, zh_peer))
        output_second(p - 1)
        if p == 1:
            spread(Uall, 1, far)
            spread(Uall, 2, near)
            arrive(b_copies)
            ready_d(0, forward(Dall, 0))
            spread(Uall, 2, far)
            u02 = forward(Uall, 1)
        if p == 2:
            spread(Uall, 4, near)
            spread(Uall, 4, far)
            ready_d(1, d2)
            spread(Uall, 5, near)
            u03 = forward(Uall, 3)
        if p == 3:
            ready_d(2, d3)

        drain()
        a_copies = []
        for ch in range(NC):
            arrive(h_copies[ch])
            right = jnp.concatenate([bR[slot, p - 1, ch] for slot in range(8)], axis=1)
            CY[p - 1, ch, y] = right - total(H.at[p - 1, ch])
            a_copies.append(share(CY.at[p - 1, ch], y, y_peer))
        if p == 1:
            spread(Dall, 1, near)
            u12 = forward(Uall, 2)
        if p == 2:
            spread(Uall, 5, far)
            u13 = forward(Uall, 4)

        drain()
        z_copies = []
        for ch in range(NC):
            arrive(a_copies[ch])
            high, low = split(CY[p - 1, ch].reshape(KC, 1024))
            Z[p, ch, zl] = dot3(high, low, Dh[p - 1], Dl[p - 1])
            z_copies.append(share(Z.at[p, ch], zl, zl_peer))
        if p == 1:
            spread(Dall, 1, far)
            ready_u(1, u02)
            add_update(2, 0, 0, KS)
            spread(Uall, 3, near)
            ready_u(2, u12)
        if p == 2:
            spread(Dall, 2, near)
            u23 = forward(Uall, 5)
            ready_u(3, u03)
            add_update(3, 0, 0, KS)
            ready_u(4, u13)
            add_update(3, 1, 0, KS)
            spread(Dall, 2, far)
            ready_u(5, u23)
        output_third(p - 1)
        drain()

    last_x, last_core = [], []
    for ch in range(NC):
        rows = slice(ch * KC, (ch + 1) * KC)
        arrive(z_copies[ch])
        value = total(Z.at[3, ch])
        for a in range(2):
            OT[3, co, x, a, rows] = value[:, a * 128 : (a + 1) * 128]
        piece = OT.at[3, co, x, :, pl.ds(ch * KC, KC)]
        last_x.append([send(piece, piece, x_peer[k]) for k in order])
    for ch in range(NC):
        arrive(last_x[ch])
        piece = OT.at[3, co, :, :, pl.ds(ch * KC, KC)]
        last_core.append([send(piece, piece, core_peer)])
    for ch in range(NC):
        arrive(last_core[ch])
    output_third(3)
    for copy in started[marks[-4] :]:
        copy.wait_send()
    for copy in stores:
        copy.wait()


def count_sends():
    return NC + 3 * NC + 7 + 9 * 4 + 1 + 3 + 4 * 3 * NC + 9 * 3 * NC + 3 * 4 + 4 * NC


def shards(factor, diag_inverse, right_side):
    sends = count_sends()
    solved = pl.pallas_call(
        kernel,
        out_shape=pltpu.VMEM((4, 2, 2, 4, 64, 128), F32),
        in_specs=[pl.BlockSpec(memory_space=pl.ANY)] * 3,
        out_specs=pl.BlockSpec(memory_space=pltpu.VMEM),
        scratch_shapes=[
            pltpu.VMEM((3072, 128), F32),
            pltpu.VMEM((1024, 128), F32),
            pltpu.VMEM((4, 128, 512), F32),
            pltpu.VMEM((3, 512, 128), F32),
            pltpu.VMEM((8, 3, NC, YC, 128), F32),
            pltpu.VMEM((8, 3, NC, YC, 128), F32),
            pltpu.VMEM((6, 2, 4, 256, 128), F32),
            pltpu.VMEM((3, 2, 4, 128, 256), F32),
            pltpu.VMEM((6, 256, 1024), BF16),
            pltpu.VMEM((6, 256, 1024), BF16),
            pltpu.VMEM((3, 1024, 256), BF16),
            pltpu.VMEM((3, 1024, 256), BF16),
            pltpu.VMEM((2, NC, 4, KC, 256), F32),
            pltpu.VMEM((NC, 4, KC, 256), F32),
            pltpu.VMEM((NC, 3, KC, 256), F32),
            pltpu.VMEM((4, NC, 4, KC, 256), F32),
            pltpu.VMEM((3, KS, 1024), F32),
            pltpu.VMEM((3, NC, 3, YC, 1024), F32),
            pltpu.VMEM((3, NC, 4, YC, 1024), F32),
            pltpu.VMEM((3, NC, 4, YC, 1024), F32),
            pltpu.VMEM((4, KS, 256), F32),
            pltpu.VMEM((4, 2, 4, 2, 64, 128), F32),
            pltpu.SemaphoreType.DMA((11,)),
            pltpu.SemaphoreType.DMA((sends,)),
            pltpu.SemaphoreType.DMA((sends,)),
            pltpu.SemaphoreType.REGULAR,
        ],
        compiler_params=pltpu.CompilerParams(
            collective_id=0, has_side_effects=True, vmem_limit_bytes=56 * 1024 * 1024
        ),
        name="substitution",
    )(
        factor.reshape(4096, 128),
        diag_inverse.reshape(1024, 128),
        right_side.reshape(4, 128, 512),
    )
    pieces = solved.reshape(8, 512, 128).transpose(0, 2, 1)
    return pieces.reshape(8, 1, 128, 512)


def solution(mesh):
    return jax.shard_map(
        shards,
        mesh=mesh,
        in_specs=(
            P(None, "row", None, None, "col", None),
            P(None, None, "col", None, None, "row", None),
            P(None, "col", None, None),
        ),
        out_specs=P(None, "row", None, None),
        check_vma=False,
    )
```
